32 devices in a mesh: group: 4 (over y, core), dev: 8 (over z, x).
Axes of the slice: x: 2, y: 2, z: 4, core: 2. Of those that a mesh axis runs over, the one named last changes fastest.
Arguments:
- node_state: bfloat16 [16384, 512], P(('group', 'dev')), may hold values from -6 to 6
- hub_state: bfloat16 [64, 512], P('dev'), may hold values from -6 to 6
- w_edge_in: bfloat16 [512, 256], replicated, may hold values from -0.25 to 0.25
- w_edge_out: bfloat16 [256, 512], replicated, may hold values from -0.375 to 0.375
- w_update: bfloat16 [512, 512], replicated, may hold values from -0.25 to 0.25
- edge_src: int32 [131072], P(('group', 'dev')), may hold values from 0 to 319
- edge_dst: int32 [131072], P(('group', 'dev')), may hold values from 0 to 319
- edge_mask: int32 [131072], P(('group', 'dev')), may hold values 0 or 1
- send_list: int32 [32, 8, 32], P(('group', 'dev')), may hold values from 0 to 511
- send_count: int32 [32, 8], P(('group', 'dev')), may hold values from 8 to 32, as said below
- node_cot: bfloat16 [16384, 512], P(('group', 'dev')), may hold values from -0.059814453 to 0.059814453
- hub_cot: bfloat16 [64, 512], P('dev'), may hold values from -0.059814453 to 0.059814453
Outputs:
- new_state: bfloat16 [16384, 512], P(('group', 'dev'))
- new_hub: bfloat16 [64, 512], P('dev')
- grad_in: float32 [512, 256], replicated
- grad_out: float32 [256, 512], replicated
- grad_update: float32 [512, 512], replicated
The draws below stay inside these ranges and needn't reach their ends.
Inputs may be any that keep to these rules, and one draw needn't show every extreme that they name: Device 0 sends 32 live slots to peer 0: send_count[0, 0] = 32.
All inputs are finite; a program needn't handle non-finite values. No bound on the sum of `edge_mask` on one device may be relied on, other than what follows from the above.
Results may differ from the reference program's by a relative error of at most 0.0064.
The reference program's roundings to bfloat16 on the way count: a program that leaves them out, or rounds other values in their place, can miss the bound.
Values may be sent and summed in bfloat16 or wider, within the bound.
No kernel may reach another device: no remote copies, remote signals or barrier semaphores. Data moves between devices by JAX's collectives and lax.ppermute only.
A program may use at most 64 MiB of HBM per device.

```python
import jax
import jax.numpy as jnp
from jax import lax

D = 512
HID = 256
E_DEV = 4096
V_DEV = 512
SLOT = 32
MIRRORS = 256
HUBS = 64
LOCAL = 320
V = 16384
EDGES = 131072
N_GROUP = 4
N_DEV = 8
DEVICES = 32


def draw_send_count(key, part):
    counts = jax.random.randint(key, (DEVICES, N_DEV), (SLOT + 3) // 4, SLOT + 1, dtype=jnp.int32)
    return counts.at[0, 0].set(SLOT)


def place_ends(values, rng, smallest, top_value):
    place = [jax.random.randint(jax.random.fold_in(rng, axis), (), 0, length) for axis, length in enumerate(values.shape)]
    longest = values.shape.index(max(values.shape))
    beside = place[:longest] + [(place[longest] + 1) % values.shape[longest]] + place[longest + 1:]
    return values.at[tuple(place)].set(smallest).at[tuple(beside)].set(top_value)


def level_of(rng, dims, pieces, low, high):
    gain = 1.0
    for dim, shards_of in pieces:
        steps = jax.random.uniform(jax.random.fold_in(jax.random.fold_in(rng, 6), dim), (shards_of,), jnp.float32, low / len(pieces), high / len(pieces))
        gain = gain * jnp.repeat(jnp.exp(steps), dims[dim] // shards_of).reshape((-1,) + (1,) * (len(dims) - 1 - dim))
    return gain


def gaussian(own_key, shape, scale, most, pieces=(), held_as=jnp.bfloat16):
    result = jax.random.normal(own_key, shape, jnp.float32) * scale
    if len(pieces) > 0:
        result = level_of(own_key, shape, pieces, -0.22, 0.18) * result
    return jnp.clip(result, min=-most, max=most).astype(held_as)


def setup_inputs(seed: int = 0) -> dict:
    key_of = jax.random.split(jax.random.key(seed), 13)
    return {
        "node_state": gaussian(key_of[0], (V, D), 1.0, 6.0, ((0, 32),)),
        "hub_state": gaussian(key_of[1], (HUBS, D), 1.0, 6.0, ((0, 8),)),
        "w_edge_in": gaussian(key_of[2], (D, HID), D ** -0.5, 0.25),
        "w_edge_out": gaussian(key_of[3], (HID, D), HID ** -0.5, 0.375),
        "w_update": gaussian(key_of[4], (D, D), D ** -0.5, 0.25),
        "edge_src": place_ends(jax.random.randint(key_of[5], (EDGES,), 0, LOCAL), jax.random.fold_in(key_of[5], 1), 0, LOCAL - 1).astype(jnp.int32),
        "edge_dst": place_ends(jax.random.randint(key_of[6], (EDGES,), 0, LOCAL), jax.random.fold_in(key_of[6], 1), 0, LOCAL - 1).astype(jnp.int32),
        "edge_mask": place_ends((jax.random.randint(key_of[7], (EDGES,), 0, 8) < 7).astype(jnp.int32), jax.random.fold_in(key_of[7], 1), 0, 1),
        "send_list": place_ends(jax.random.randint(key_of[8], (DEVICES, N_DEV, SLOT), 0, V_DEV), jax.random.fold_in(key_of[8], 1), 0, V_DEV - 1).astype(jnp.int32),
        "send_count": draw_send_count(jax.random.fold_in(key_of[12], 71), 0),
        "node_cot": gaussian(key_of[10], (V, D), 0.01, 0.059814453, ((0, 32),)),
        "hub_cot": gaussian(key_of[11], (HUBS, D), 0.01, 0.059814453, ((0, 8),)),
    }


def silu_grad(values):
    sigmoid_v = jax.nn.sigmoid(values)
    return sigmoid_v * (1.0 + values * (1.0 - sigmoid_v))

def finish(states, summed, degree, w_update):
    mean_part = summed / jnp.maximum(degree, 1.0)[:, None]
    mixed_rows = (states.astype(jnp.float32) + mean_part).astype(jnp.bfloat16)
    pre_update = jnp.dot(mixed_rows, w_update, preferred_element_type=jnp.float32)
    updated = (states.astype(jnp.float32) + jax.nn.silu(pre_update)).astype(jnp.bfloat16)
    return (mixed_rows, pre_update, updated)

def backward_rows(cotangent, pre_update, degree, w_update):
    grad_pre = (cotangent.astype(jnp.float32) * silu_grad(pre_update)).astype(jnp.bfloat16)
    grad_mix = jnp.dot(grad_pre, w_update.T, preferred_element_type=jnp.float32)
    grad_sum = (grad_mix / jnp.maximum(degree, 1.0)[:, None]).astype(jnp.bfloat16)
    return (grad_pre, grad_sum)

def pick_rows(states, send_rows):
    return states[send_rows]

def spread(source, send_rows, live_slot, hub_rows):
    per_master = source.reshape(N_GROUP, N_DEV, V_DEV, D)
    picked = jax.vmap(jax.vmap(pick_rows))(per_master, send_rows)
    picked = jnp.where(live_slot[..., None], picked, jnp.zeros((), jnp.bfloat16))
    mirrors = jnp.swapaxes(picked, 1, 2).reshape(N_GROUP, N_DEV, MIRRORS, D)
    hub_table = jnp.broadcast_to(hub_rows, (N_GROUP, N_DEV, HUBS, D))
    return jnp.concatenate([mirrors, hub_table], axis=2).reshape(N_GROUP * N_DEV, LOCAL, D)

def collect(values, counts, send_rows):
    flat_rows = send_rows.reshape(-1)
    summed = jnp.zeros((V_DEV, D), jnp.float32).at[flat_rows].add(values.reshape(-1, D))
    degree = jnp.zeros((V_DEV,), jnp.float32).at[flat_rows].add(counts.reshape(-1))
    return (summed, degree)

def reference(node_state, hub_state, w_edge_in, w_edge_out, w_update, edge_src, edge_dst, edge_mask, send_list, send_count, node_cot, hub_cot):
    peer_count = N_GROUP * N_DEV
    send_rows = send_list.reshape(N_GROUP, N_DEV, N_DEV, SLOT)
    live_slot = jnp.arange(SLOT)[None, None, None, :] < send_count.reshape(N_GROUP, N_DEV, N_DEV)[..., None]
    tables = spread(node_state, send_rows, live_slot, hub_state)
    sources = edge_src.reshape(peer_count, E_DEV)
    targets = edge_dst.reshape(peer_count, E_DEV)
    edge_keep = edge_mask.reshape(peer_count, E_DEV)

    def edge_forward(inputs):
        local_table, source_ids, target_ids, keep_ids = inputs
        gathered = local_table[source_ids]
        pre_act = jnp.dot(gathered, w_edge_in, preferred_element_type=jnp.float32)
        hidden = jax.nn.silu(pre_act).astype(jnp.bfloat16)
        message = jnp.dot(hidden, w_edge_out, preferred_element_type=jnp.float32) * keep_ids[:, None].astype(jnp.float32)
        message = message.astype(jnp.bfloat16).astype(jnp.float32)
        partial_value = jnp.zeros((LOCAL, D), jnp.float32).at[target_ids].add(message)
        counts = jnp.zeros((LOCAL,), jnp.float32).at[target_ids].add(keep_ids.astype(jnp.float32))
        return (partial_value, counts)
    partials, counts = lax.map(edge_forward, (tables, sources, targets, edge_keep))
    mirror_part = lax.optimization_barrier(partials[:, :MIRRORS].astype(jnp.bfloat16)).astype(jnp.float32)
    mirror_count = lax.optimization_barrier(counts[:, :MIRRORS].astype(jnp.bfloat16)).astype(jnp.float32)
    mirror_part = jnp.swapaxes(mirror_part.reshape(N_GROUP, N_DEV, N_DEV, SLOT, D), 1, 2)
    mirror_count = jnp.swapaxes(mirror_count.reshape(N_GROUP, N_DEV, N_DEV, SLOT), 1, 2)
    mirror_part = mirror_part * live_slot[..., None].astype(jnp.float32)
    mirror_count = mirror_count * live_slot.astype(jnp.float32)
    summed, degree = jax.vmap(jax.vmap(collect))(mirror_part, mirror_count, send_rows)
    summed = summed.reshape(V_DEV * peer_count, D)
    degree = degree.reshape(V_DEV * peer_count)
    hub_summed = lax.optimization_barrier(jnp.sum(partials[:, MIRRORS:], axis=0))
    hub_degree = lax.optimization_barrier(jnp.sum(counts[:, MIRRORS:], axis=0))
    mixed_rows, pre_update, new_state = finish(node_state, summed, degree, w_update)
    hub_mixed, hub_pre, new_hub = finish(hub_state, hub_summed, hub_degree, w_update)
    grad_pre, grad_sum = backward_rows(node_cot, pre_update, degree, w_update)
    hub_grad_pre, hub_grad_sum = backward_rows(hub_cot, hub_pre, hub_degree, w_update)
    contract = (((0,), (0,)), ((), ()))
    grad_update = lax.dot_general(mixed_rows, grad_pre, contract, preferred_element_type=jnp.float32)
    grad_update = grad_update + lax.dot_general(hub_mixed, hub_grad_pre, contract, preferred_element_type=jnp.float32)
    grad_tables = spread(grad_sum, send_rows, live_slot, hub_grad_sum)

    def edge_backward(totals, inputs):
        local_table, grad_table, source_ids, target_ids, keep_ids = inputs
        gathered = local_table[source_ids]
        pre_act = jnp.dot(gathered, w_edge_in, preferred_element_type=jnp.float32)
        hidden = jax.nn.silu(pre_act).astype(jnp.bfloat16)
        grad_message = jnp.where(keep_ids[:, None] > 0, grad_table[target_ids], jnp.zeros((), jnp.bfloat16))
        grad_w_out = lax.dot_general(hidden, grad_message, contract, preferred_element_type=jnp.float32)
        grad_hidden = jnp.dot(grad_message, w_edge_out.T, preferred_element_type=jnp.float32)
        grad_act = (grad_hidden * silu_grad(pre_act)).astype(jnp.bfloat16)
        grad_w_in = lax.dot_general(gathered, grad_act, contract, preferred_element_type=jnp.float32)
        return ((totals[0] + grad_w_in, totals[1] + grad_w_out), None)
    start = (jnp.zeros((D, HID), jnp.float32), jnp.zeros((HID, D), jnp.float32))
    grads, _ = lax.scan(edge_backward, start, (tables, grad_tables, sources, targets, edge_keep))
    return (new_state, new_hub, grads[0], grads[1], grad_update)
```

```python
import jax
import jax.numpy as jnp
from jax import lax
from jax.sharding import PartitionSpec as P

F32 = jnp.float32
BF16 = jnp.bfloat16


def silu_grad(values):
    sigmoid_v = jax.nn.sigmoid(values)
    return sigmoid_v * (1.0 + values * (1.0 - sigmoid_v))


def dot(left, right, dims=((1,), (0,))):
    return lax.dot_general(left, right, (dims, ((), ())), preferred_element_type=F32)


def split_dot(left, right, dims):
    high = left.astype(BF16)
    low = (left - high.astype(F32)).astype(BF16)
    return dot(high, right, dims) + dot(low, right, dims)


def swap(blocks, axis, size, stride, total):
    position = lax.rem(lax.div(lax.axis_index(axis), stride), size)
    if size == 2:
        pairs = [(i, i ^ stride) for i in range(total)]
        other = lax.ppermute(lax.dynamic_index_in_dim(blocks, 1 - position, 0, False), axis, pairs)
        own = lax.dynamic_index_in_dim(blocks, position, 0, False)
        first = position == 0
        return jnp.stack([jnp.where(first, own, other), jnp.where(first, other, own)])
    if size * stride == total and stride == 1:
        groups = None
    else:
        groups = [
            [base + off + i * stride for i in range(size)]
            for base in range(0, total, size * stride)
            for off in range(stride)
        ]
    return lax.all_to_all(blocks, axis, 0, 0, tiled=True, axis_index_groups=groups)


def scatter_sum(value, axis, size, stride, total):
    position = lax.rem(lax.div(lax.axis_index(axis), stride), size)
    blocks = value.reshape(size, -1, value.shape[1])
    if size == 2:
        pairs = [(i, i ^ stride) for i in range(total)]
        sent = lax.dynamic_index_in_dim(blocks, 1 - position, 0, False).astype(BF16)
        own = lax.dynamic_index_in_dim(blocks, position, 0, False)
        return own + lax.ppermute(sent, axis, pairs).astype(F32)
    return jnp.sum(swap(blocks.astype(BF16), axis, size, stride, total).astype(F32), axis=0)


def gather_all(value, axis, size, stride, total):
    spread = jnp.broadcast_to(value[None], (size,) + value.shape)
    return swap(spread, axis, size, stride, total).reshape(-1, value.shape[1])


def shards(
    node_state,
    hub_state,
    w_edge_in,
    w_edge_out,
    w_update,
    edge_src,
    edge_dst,
    edge_mask,
    send_list,
    send_count,
    node_cot,
    hub_cot,
    *,
    n_group,
    n_dev,
):
    width = node_state.shape[1]
    hidden_width = w_edge_in.shape[1]
    master_rows = node_state.shape[0]
    send_rows = send_list[0]
    slot_width = send_rows.shape[1]
    mirror_total = n_dev * slot_width
    hub_rows = hub_state.shape[0]
    live_slot = jnp.arange(slot_width)[None, :] < send_count[0][:, None]
    chosen = jnp.where(live_slot, send_rows, -1).reshape(1, -1)
    select = (jnp.arange(master_rows)[:, None] == chosen).astype(BF16)

    outgoing = dot(select, node_state, ((0,), (0,))).astype(BF16)
    packed = jnp.concatenate(
        [
            outgoing.reshape(n_dev, slot_width, width),
            jnp.broadcast_to(hub_state[None], (n_dev, hub_rows, width)),
        ],
        axis=1,
    )
    arrived = lax.all_to_all(packed, "dev", 0, 0, tiled=True)
    table = jnp.concatenate(
        [
            arrived[:, :slot_width].reshape(mirror_total, width),
            arrived[:, slot_width:].reshape(-1, width),
        ],
        axis=0,
    )
    local_rows = table.shape[0]

    ids = jnp.arange(local_rows)[:, None]
    from_hot = (ids == edge_src[None, :]).astype(BF16)
    to_hot = (ids == jnp.where(edge_mask > 0, edge_dst, -1)[None, :]).astype(BF16)
    adjacency = dot(to_hot, from_hot, ((1,), (1,)))
    adj_high = jnp.floor(adjacency * (1.0 / 256.0))
    adj_low = (adjacency - 256.0 * adj_high).astype(BF16)
    adj_high = adj_high.astype(BF16)
    counts = jnp.sum(adjacency, axis=1)

    pre_act = dot(table, w_edge_in)
    hidden = jax.nn.silu(pre_act).astype(BF16)
    partial = dot(adj_low, hidden) + 256.0 * dot(adj_high, hidden)

    def by_peer(value, hubs_of):
        return jnp.concatenate(
            [
                value[:mirror_total].reshape((n_dev, slot_width) + value.shape[1:]),
                value[mirror_total:].reshape((n_dev, hubs_of) + value.shape[1:]),
            ],
            axis=1,
        )

    rounded_count = counts.astype(BF16)
    rest_count = (counts - rounded_count.astype(F32)).astype(BF16)
    count_rows = jnp.stack([by_peer(rounded_count, hub_rows), by_peer(rest_count, hub_rows)], axis=1)
    count_rows = jnp.pad(
        count_rows, ((0, 0), (0, 6), (0, hidden_width - slot_width - hub_rows))
    )
    message = jnp.concatenate([by_peer(partial.astype(BF16), hub_rows), count_rows], axis=1)
    back = lax.all_to_all(message, "dev", 0, 0, tiled=True)
    base = slot_width + hub_rows
    back_part = back[:, :slot_width].reshape(mirror_total, hidden_width)
    back_count = back[:, base, :slot_width].reshape(mirror_total, 1)
    summed_hidden = dot(select, back_part)
    degree = dot(select, back_count)
    hub_hidden = jnp.sum(back[:, slot_width:base].astype(F32), axis=0)
    hub_degree = jnp.sum(back[:, base : base + 2, slot_width:base].astype(F32), axis=(0, 1))
    hub_sums = jnp.concatenate(
        [hub_hidden, jnp.broadcast_to(hub_degree[:, None], (hub_rows, 128))], axis=1
    )
    hub_sums = lax.psum(hub_sums, "group")
    hub_hidden, hub_degree = hub_sums[:, :hidden_width], hub_sums[:, hidden_width : hidden_width + 1]

    states = jnp.concatenate([node_state, hub_state], axis=0).astype(F32)
    cotangent = jnp.concatenate([node_cot, hub_cot], axis=0).astype(F32)
    degree = jnp.maximum(jnp.concatenate([degree, hub_degree], axis=0), 1.0)
    summed_hidden = jnp.concatenate([summed_hidden, hub_hidden], axis=0)
    summed = split_dot(summed_hidden, w_edge_out, ((1,), (0,)))
    mixed = (states + summed / degree).astype(BF16)
    pre_update = dot(mixed, w_update)
    updated = (states + jax.nn.silu(pre_update)).astype(BF16)
    grad_pre = (cotangent * silu_grad(pre_update)).astype(BF16)
    grad_sum = (dot(grad_pre, w_update, ((1,), (1,))) / degree).astype(BF16)
    grad_hidden = dot(grad_sum, w_edge_out, ((1,), (1,))).astype(BF16)

    grad_outgoing = dot(select, grad_hidden[:master_rows], ((0,), (0,))).astype(BF16)
    packed_grad = jnp.concatenate(
        [
            grad_outgoing.reshape(n_dev, slot_width, hidden_width),
            jnp.broadcast_to(grad_hidden[None, master_rows:], (n_dev, hub_rows, hidden_width)),
        ],
        axis=1,
    )
    arrived_grad = lax.all_to_all(packed_grad, "dev", 0, 0, tiled=True)
    grad_rows = jnp.concatenate(
        [
            arrived_grad[:, :slot_width].reshape(mirror_total, hidden_width),
            arrived_grad[:, slot_width:].reshape(-1, hidden_width),
        ],
        axis=0,
    )

    row_weight = jnp.where(
        jnp.arange(mixed.shape[0])[:, None] < master_rows,
        1.0,
        (lax.axis_index("group") == 0).astype(F32),
    )
    weighted = (grad_pre.astype(F32) * row_weight).astype(BF16)
    grad_update = dot(mixed, weighted, ((0,), (0,)))
    grad_out = split_dot(summed_hidden * row_weight, grad_sum, ((0,), (0,)))

    by_source = dot(adj_low, grad_rows, ((0,), (0,))) + 256.0 * dot(
        adj_high, grad_rows, ((0,), (0,))
    )
    grad_act = by_source * silu_grad(pre_act)
    act_high = grad_act.astype(BF16)
    act_low = (grad_act - act_high.astype(F32)).astype(BF16)
    grad_in = dot(table, act_high, ((0,), (0,))) + dot(table, act_low, ((0,), (0,)))

    half = width // 2
    side = jnp.concatenate([grad_in[:half], grad_in[half:]], axis=1)
    whole = jnp.concatenate([grad_update, grad_out, side], axis=0)
    whole = scatter_sum(whole, "group", 2, 1, n_group)
    whole = scatter_sum(whole, "group", n_group // 2, 2, n_group)
    whole = scatter_sum(whole, "dev", n_dev, 1, n_dev)
    whole = gather_all(whole.astype(BF16), "dev", n_dev, 1, n_dev)
    whole = gather_all(whole, "group", n_group // 2, 2, n_group)
    whole = gather_all(whole, "group", 2, 1, n_group).astype(F32)
    side = whole[width + hidden_width :]
    return (
        updated[:master_rows],
        updated[master_rows:],
        jnp.concatenate([side[:, :hidden_width], side[:, hidden_width:]], axis=0),
        whole[width : width + hidden_width],
        whole[:width],
    )


def solution(mesh):
    def body(*args):
        return shards(*args, n_group=mesh.shape["group"], n_dev=mesh.shape["dev"])

    return jax.shard_map(
        body,
        mesh=mesh,
        in_specs=(
            P(("group", "dev"), None),
            P("dev", None),
            P(),
            P(),
            P(),
            P(("group", "dev")),
            P(("group", "dev")),
            P(("group", "dev")),
            P(("group", "dev"), None, None),
            P(("group", "dev"), None),
            P(("group", "dev"), None),
            P("dev", None),
        ),
        out_specs=(P(("group", "dev"), None), P("dev", None), P(), P(), P()),
        check_vma=False,
    )
```

```python
import functools

import jax
import jax.numpy as jnp
from jax import lax
from jax.experimental import pallas as pl
from jax.experimental.pallas import tpu as pltpu
from jax.sharding import PartitionSpec as P

F32 = jnp.float32
BF16 = jnp.bfloat16
I32 = jnp.int32
NN = ((1,), (0,))
NT = ((1,), (1,))
TN = ((0,), (0,))


def dot(left, right, dims=NN):
    return lax.dot_general(left, right, (dims, ((), ())), preferred_element_type=F32)


def halves(value):
    high = value.astype(BF16)
    return high, (value - high.astype(F32)).astype(BF16)


def silu(values):
    return values * jax.nn.sigmoid(values)


def silu_grad(values):
    sigmoid_v = jax.nn.sigmoid(values)
    return sigmoid_v * (1.0 + values * (1.0 - sigmoid_v))


def iota(shape, axis):
    return lax.broadcasted_iota(I32, shape, axis)


class Layout:
    def __init__(self, peers, slots, hubs):
        self.peers, self.slots, self.hubs = peers, slots, hubs
        self.base = slots + hubs
        self.block = -(-(self.base + 2) // 16) * 16
        self.rows = peers * self.block

    def place(self, ids):
        mirrors = self.peers * self.slots
        slot_bits, hub_bits = self.slots.bit_length() - 1, self.hubs.bit_length() - 1
        hub_ids = ids - mirrors
        mirror_row = (ids >> slot_bits) * self.block + (ids & (self.slots - 1))
        hub_row = (hub_ids >> hub_bits) * self.block + self.slots + (hub_ids & (self.hubs - 1))
        return jnp.where(ids < mirrors, mirror_row, hub_row)


def gather_body(lay, chosen_ref, rows_ref, hubs_ref, out_ref):
    rows = rows_ref.shape[0]
    select = (iota((rows, lay.rows), 0) == chosen_ref[...]).astype(BF16)
    picked = dot(select, rows_ref[...], TN)
    hubs = hubs_ref[...].astype(F32)
    rest = jnp.zeros((lay.block - lay.base, hubs.shape[1]), F32)
    for peer in range(lay.peers):
        start = peer * lay.block
        part = [picked[start : start + lay.slots], hubs, rest]
        out_ref[start : start + lay.block, :] = jnp.concatenate(part, axis=0).astype(BF16)


def count_body(
    lay, src_ref, dst_ref, mask_ref, low_ref, high_ref, low_t_ref, high_t_ref, rows_ref, sum_ref
):
    steps, chunk = src_ref.shape
    ids = iota((lay.rows, chunk), 0)
    for step in range(steps):
        src = lay.place(src_ref[step : step + 1, :])
        keep = mask_ref[step : step + 1, :] > 0
        dst = jnp.where(keep, lay.place(dst_ref[step : step + 1, :]), -1)
        added = dot((ids == dst).astype(BF16), (ids == src).astype(BF16), NT)
        if step == 0:
            sum_ref[...] = added
        else:
            sum_ref[...] += added
    total = sum_ref[...]
    high = jnp.floor(total * (1.0 / 256.0))
    low = total - 256.0 * high
    low_ref[...] = low.astype(BF16)
    high_ref[...] = high.astype(BF16)
    low_t_ref[...] = low.T.astype(BF16)
    high_t_ref[...] = high.T.astype(BF16)
    counts = jnp.sum(total.T, axis=0, keepdims=True)
    rounded = counts.astype(BF16).astype(F32)
    shape = (lay.rows, lay.rows)
    row, col = iota(shape, 0), iota(shape, 1)
    row_block = jnp.floor((row.astype(F32) + 0.5) * (1.0 / lay.block))
    col_block = jnp.floor((col.astype(F32) + 0.5) * (1.0 / lay.block))
    row_rest = row.astype(F32) - lay.block * row_block
    same = row_block == col_block
    spread = jnp.where(same & (row_rest == lay.base), rounded, 0.0)
    spread += jnp.where(same & (row_rest == lay.base + 1), counts - rounded, 0.0)
    shape = (lay.rows, rows_ref.shape[1])
    row = iota(shape, 0).astype(F32)
    row_rest = row - lay.block * jnp.floor((row + 0.5) * (1.0 / lay.block))
    fold = (row_rest == iota(shape, 1).astype(F32)).astype(BF16)
    rows_ref[...] = dot(spread.astype(BF16), fold).astype(BF16)


def forward_body(table_ref, w_ref, low_ref, high_ref, rows_ref, out_ref):
    hidden = silu(dot(table_ref[...], w_ref[...])).astype(BF16)
    partial = dot(low_ref[...], hidden) + 256.0 * dot(high_ref[...], hidden)
    out_ref[...] = (partial + rows_ref[...].astype(F32)).astype(BF16)


def slope_body(n_group, n_dev, table_ref, w_ref, slope_ref, table_t_ref):
    slope_ref[...] = silu_grad(dot(table_ref[...], w_ref[...]))
    width = table_ref.shape[1]
    depth = width // (n_group * n_dev)
    depth_bits, dev_bits = depth.bit_length() - 1, n_dev.bit_length() - 1
    row = iota((width, width), 0)
    block = row >> depth_bits
    group, dev = block >> dev_bits, block & (n_dev - 1)
    order = (group & 1) * (n_group // 2) + (group >> 1)
    order = (order * 2 + (dev & 1)) * (n_dev // 2) + (dev >> 1)
    source = order * depth + (row & (depth - 1))
    turn = (iota((width, width), 1) == source).astype(BF16)
    table_t_ref[...] = dot(turn, table_ref[...], NT).astype(BF16)


def hub_sum_body(lay, back_ref, out_ref):
    width = back_ref.shape[1]
    hidden = jnp.zeros((lay.hubs, width), F32)
    counts = jnp.zeros((lay.block - lay.base, width), F32)
    for peer in range(lay.peers):
        start = peer * lay.block
        part = back_ref[start + lay.slots : start + lay.block, :].astype(F32)
        hidden += part[: lay.hubs]
        counts += part[lay.hubs :]
    count = counts[0:1] + counts[1:2]
    shape = (lay.hubs, width)
    own = iota(shape, 1) == iota(shape, 0) + lay.slots
    degree = jnp.sum(jnp.where(own, count, 0.0), axis=1, keepdims=True)
    out_ref[:, :width] = hidden
    out_ref[:, width:] = jnp.broadcast_to(degree, (lay.hubs, out_ref.shape[1] - width))


def update_rows(states, cotangent, hidden_sum, degree, w_out, w_update):
    high, low = halves(hidden_sum)
    share = 1.0 / jnp.maximum(degree, 1.0)
    mixed = (states + (dot(high, w_out) + dot(low, w_out)) * share).astype(BF16)
    pre = dot(mixed, w_update)
    updated = (states + silu(pre)).astype(BF16)
    grad_pre = (cotangent * silu_grad(pre)).astype(BF16)
    grad_sum = (dot(grad_pre, w_update, NT) * share).astype(BF16)
    grad_hidden = dot(grad_sum, w_out, NT).astype(BF16)
    return updated, mixed, grad_pre, high, low, grad_sum, grad_hidden


def master_body(
    lay,
    chosen_ref,
    back_ref,
    state_ref,
    cot_ref,
    w_out_ref,
    w_up_ref,
    new_ref,
    mixed_ref,
    pre_ref,
    high_ref,
    low_ref,
    sum_ref,
    out_ref,
):
    width = back_ref.shape[1]
    select = (iota((state_ref.shape[0], lay.rows), 0) == chosen_ref[...]).astype(BF16)
    back = back_ref[...]
    shape = (lay.rows, lay.rows)
    row, col = iota(shape, 0).astype(F32), iota(shape, 1).astype(F32)
    row_block = jnp.floor((row + 0.5) * (1.0 / lay.block))
    taken = (col == row_block * lay.block + lay.base).astype(BF16)
    shape = (lay.rows, width)
    row = iota(shape, 0).astype(F32)
    row_rest = row - lay.block * jnp.floor((row + 0.5) * (1.0 / lay.block))
    counts = jnp.where(row_rest == iota(shape, 1).astype(F32), dot(taken, back), 0.0)
    degree = jnp.sum(dot(select, counts.astype(BF16)), axis=1, keepdims=True)
    results = update_rows(
        state_ref[...].astype(F32),
        cot_ref[...].astype(F32),
        dot(select, back),
        degree,
        w_out_ref[...],
        w_up_ref[...],
    )
    updated, mixed, grad_pre, high, low, grad_sum, grad_hidden = results
    new_ref[...] = updated
    mixed_ref[...] = mixed
    pre_ref[...] = grad_pre
    high_ref[...] = high
    low_ref[...] = low
    sum_ref[...] = grad_sum
    out_ref[...] = dot(select, grad_hidden, TN)


def hub_body(
    lay,
    n_parts,
    *refs,
):
    parts = refs[:n_parts]
    state_ref, cot_ref, w_out_ref, w_up_ref, rows_ref = refs[n_parts : n_parts + 5]
    new_ref, mixed_ref, pre_ref, high_ref, low_ref, sum_ref, out_ref = refs[n_parts + 5 :]
    total = parts[0][...]
    for part in parts[1:]:
        total += part[...]
    width = rows_ref.shape[1]
    results = update_rows(
        state_ref[...].astype(F32),
        cot_ref[...].astype(F32),
        total[:, :width],
        total[:, width : width + 1],
        w_out_ref[...],
        w_up_ref[...],
    )
    updated, mixed, grad_pre, high, low, grad_sum, grad_hidden = results
    new_ref[...] = updated
    mixed_ref[...] = mixed
    pre_ref[...] = grad_pre
    high_ref[...] = high
    low_ref[...] = low
    sum_ref[...] = grad_sum
    hubs = grad_hidden.astype(F32)
    rest = jnp.zeros((lay.block - lay.base, width), F32)
    for peer in range(lay.peers):
        start = peer * lay.block
        part = [rows_ref[start : start + lay.slots, :], hubs, rest]
        out_ref[start : start + lay.block, :] = jnp.concatenate(part, axis=0).astype(BF16)


def weight_body(
    weight_ref,
    mixed_ref,
    pre_ref,
    high_ref,
    low_ref,
    sum_ref,
    hub_mixed_ref,
    hub_pre_ref,
    hub_high_ref,
    hub_low_ref,
    hub_sum_ref,
    out_ref,
):
    weight = weight_ref[0].astype(F32)
    rows = mixed_ref.shape[1]
    grad_sum, hub_grad = sum_ref[...], hub_sum_ref[...]
    out_ref[:rows, :] = dot(mixed_ref[...], pre_ref[...], TN) + weight * dot(
        hub_mixed_ref[...], hub_pre_ref[...], TN
    )
    hub_part = dot(hub_high_ref[...], hub_grad, TN) + dot(hub_low_ref[...], hub_grad, TN)
    main = dot(high_ref[...], grad_sum, TN) + dot(low_ref[...], grad_sum, TN)
    out_ref[rows:, :] = main + weight * hub_part


def backward_body(grad_ref, low_ref, high_ref, slope_ref, table_t_ref, out_ref):
    grad = grad_ref[...]
    by_source = dot(low_ref[...], grad) + 256.0 * dot(high_ref[...], grad)
    high, low = halves(by_source * slope_ref[...])
    table_t = table_t_ref[...]
    out_ref[...] = (dot(table_t, high) + dot(table_t, low)).astype(BF16)


def call(body, outs, args, scratch=(), flops=0, smem=0):
    outs = [jax.ShapeDtypeStruct(shape, kind) for shape, kind in outs]
    moved = sum(a.size * a.dtype.itemsize for a in list(args) + outs)
    vmem = pl.BlockSpec(memory_space=pltpu.VMEM)
    specs = [pl.BlockSpec(memory_space=pltpu.SMEM)] * smem + [vmem] * (len(args) - smem)
    single = len(outs) == 1
    return pl.pallas_call(
        body,
        out_shape=outs[0] if single else outs,
        in_specs=specs,
        out_specs=vmem if single else [vmem] * len(outs),
        scratch_shapes=list(scratch),
        compiler_params=pltpu.CompilerParams(vmem_limit_bytes=VMEM_LIMIT),
        cost_estimate=pl.CostEstimate(
            flops=int(flops), bytes_accessed=int(moved), transcendentals=0
        ),
    )(*args)


VMEM_LIMIT = 44 * 1024 * 1024


class Cube:
    def __init__(self, n_group, n_dev, parts):
        self.total = n_group * n_dev
        self.size, self.steps, self.place = 1, [0], 0
        for axis, stride, size in parts:
            unit = stride * (n_dev if axis == "group" else 1)
            place = lax.rem(lax.div(lax.axis_index(axis), stride), size)
            self.place = self.place * size + place
            self.steps = [s | (i * unit) for s in self.steps for i in range(size)]
            self.size *= size

    def send(self, value, step):
        pairs = [(i, i ^ self.steps[step]) for i in range(self.total)]
        return lax.ppermute(value, ("group", "dev"), pairs)

    def scatter(self, value):
        blocks = value.reshape(self.size, -1, value.shape[1])
        own = lax.dynamic_index_in_dim(blocks, self.place, 0, False)
        terms = []
        for step in range(1, self.size):
            block = lax.dynamic_index_in_dim(blocks, self.place ^ step, 0, False)
            terms.append(self.send(block.astype(BF16), step))
        return own, terms

    def gather(self, value):
        parts = [value] + [self.send(value, step) for step in range(1, self.size)]
        bit = 1
        while bit < self.size:
            flip = (self.place & bit) > 0
            parts = [jnp.where(flip, parts[i ^ bit], parts[i]) for i in range(self.size)]
            bit *= 2
        return jnp.concatenate(parts, axis=0)


def total(own, terms):
    for term in terms:
        own += term.astype(F32)
    return own


def shards(
    node_state,
    hub_state,
    w_edge_in,
    w_edge_out,
    w_update,
    edge_src,
    edge_dst,
    edge_mask,
    send_list,
    send_count,
    node_cot,
    hub_cot,
    *,
    n_group,
    n_dev,
):
    rows, width = node_state.shape
    hid = w_edge_in.shape[1]
    slots = send_list.shape[2]
    hubs = hub_state.shape[0]
    lay = Layout(n_dev, slots, hubs)
    both = ("group", "dev")
    live = jnp.arange(slots)[None, :] < send_count[0][:, None]
    chosen = jnp.where(live, send_list[0], -1)
    chosen = jnp.pad(chosen, ((0, 0), (0, lay.block - slots)), constant_values=-1).reshape(1, -1)

    def body(function, *static):
        return functools.partial(function, *static)

    packed = call(
        body(gather_body, lay), [((lay.rows, width), BF16)], [chosen, node_state, hub_state]
    )
    table = lax.all_to_all(packed, "dev", 0, 0, tiled=True)

    chunk = min(512, edge_src.shape[0])
    square = ((lay.rows, lay.rows), BF16)
    edges = [a.reshape(-1, chunk) for a in (edge_src, edge_dst, edge_mask)]
    low, high, low_t, high_t, count_rows = call(
        body(count_body, lay),
        [square, square, square, square, ((lay.rows, hid), BF16)],
        edges,
        scratch=[pltpu.VMEM((lay.rows, lay.rows), F32)],
        flops=2 * edge_src.shape[0] * lay.rows * lay.rows,
    )
    message = call(
        forward_body,
        [((lay.rows, hid), BF16)],
        [table, w_edge_in, low, high, count_rows],
    )
    back = lax.all_to_all(message, "dev", 0, 0, tiled=True)
    slope, table_t = call(
        body(slope_body, n_group, n_dev),
        [((lay.rows, hid), F32), ((width, lay.rows), BF16)],
        [table, w_edge_in],
        flops=2 * lay.rows * width * hid,
    )

    hub_part = call(body(hub_sum_body, lay), [((hubs, hid + 128), F32)], [back])
    group_cube = Cube(n_group, n_dev, [("group", 1, n_group)])
    parts = [hub_part] + [group_cube.send(hub_part, step) for step in range(1, n_group)]

    def row_outs(count):
        return [
            ((count, width), BF16),
            ((count, width), BF16),
            ((count, width), BF16),
            ((count, hid), BF16),
            ((count, hid), BF16),
            ((count, width), BF16),
        ]

    new_state, *saved, grad_rows = call(
        body(master_body, lay),
        row_outs(rows) + [((lay.rows, hid), F32)],
        [chosen, back, node_state, node_cot, w_edge_out, w_update],
        flops=2 * rows * (2 * lay.rows * hid + 2 * width * width + 2 * width * hid),
    )
    new_hub, *hub_saved, grad_message = call(
        body(hub_body, lay, n_group),
        row_outs(hubs) + [((lay.rows, hid), BF16)],
        parts + [hub_state, hub_cot, w_edge_out, w_update, grad_rows],
    )
    grad_table = lax.all_to_all(grad_message, "dev", 0, 0, tiled=True)

    weight = (lax.axis_index("group") == 0).astype(I32).reshape(1)
    upper = call(
        weight_body,
        [((width + hid, width), F32)],
        [weight] + saved + hub_saved,
        flops=2 * rows * width * (width + 2 * hid),
        smem=1,
    )
    side = call(
        backward_body,
        [((width, hid), BF16)],
        [grad_table, low_t, high_t, slope, table_t],
        flops=2 * lay.rows * hid * (lay.rows + width) * 2,
    )
    core = Cube(n_group, n_dev, [("group", 1, 2)])
    flat = Cube(n_group, n_dev, [("group", 2, n_group // 2), ("dev", 1, 2)])
    line = Cube(n_group, n_dev, [("dev", 2, n_dev // 2)])
    upper = total(*core.scatter(upper))
    upper, terms = flat.scatter(upper)
    terms, side = lax.optimization_barrier((terms, side))
    upper = total(upper, terms)
    upper = total(*line.scatter(upper)).astype(BF16)

    side = lax.all_to_all(side, both, 0, 0, tiled=True)
    own = jnp.sum(side.reshape(n_group * n_dev, -1, hid).astype(F32), axis=0).astype(BF16)
    depth = own.shape[0] // 2
    own = jnp.concatenate([own[:depth], own[depth:]], axis=1)
    whole = jnp.concatenate([upper, own], axis=0)
    for cube in (line, flat, core):
        whole = cube.gather(whole)
    whole = whole.reshape(n_group * n_dev, -1, width).astype(F32)
    split = whole.shape[1] - depth
    upper = whole[:, :split].reshape(-1, width)
    side = whole[:, split:]
    side = jnp.concatenate([side[:, :, :hid], side[:, :, hid:]], axis=1).reshape(width, hid)
    return new_state, new_hub, side, upper[width:], upper[:width]


def solution(mesh):
    def body(*args):
        return shards(*args, n_group=mesh.shape["group"], n_dev=mesh.shape["dev"])

    return jax.shard_map(
        body,
        mesh=mesh,
        in_specs=(
            P(("group", "dev"), None),
            P("dev", None),
            P(),
            P(),
            P(),
            P(("group", "dev")),
            P(("group", "dev")),
            P(("group", "dev")),
            P(("group", "dev"), None, None),
            P(("group", "dev"), None),
            P(("group", "dev"), None),
            P("dev", None),
        ),
        out_specs=(P(("group", "dev"), None), P("dev", None), P(), P(), P()),
        check_vma=False,
    )
```

```python
import functools

import jax
import jax.numpy as jnp
from jax import lax
from jax.experimental import pallas as pl
from jax.experimental.pallas import tpu as pltpu
from jax.sharding import PartitionSpec as P

F32 = jnp.float32
BF16 = jnp.bfloat16
I32 = jnp.int32
CHUNK = 512
NN = ((1,), (0,))
NT = ((1,), (1,))
TN = ((0,), (0,))


def dot(left, right, dims=NN):
    return lax.dot_general(left, right, (dims, ((), ())), preferred_element_type=F32)


def halves(value):
    high = value.astype(BF16)
    return high, (value - high.astype(F32)).astype(BF16)


def silu(values):
    return values * jax.nn.sigmoid(values)


def silu_grad(values):
    sigmoid_v = jax.nn.sigmoid(values)
    return sigmoid_v * (1.0 + values * (1.0 - sigmoid_v))


def iota(shape, axis):
    return lax.broadcasted_iota(I32, shape, axis)


class Layout:
    def __init__(self, peers, slots, hubs):
        self.peers, self.slots, self.hubs = peers, slots, hubs
        self.block = slots + hubs
        self.wide = -(-(self.block + 2) // 16) * 16
        self.rows, self.wide_rows = peers * self.block, peers * self.wide

    def place(self, ids):
        mirrors = self.peers * self.slots
        slot_bits, hub_bits = self.slots.bit_length() - 1, self.hubs.bit_length() - 1
        hub_ids = ids - mirrors
        mirror_row = (ids >> slot_bits) * self.block + (ids & (self.slots - 1))
        hub_row = (hub_ids >> hub_bits) * self.block + self.slots + (hub_ids & (self.hubs - 1))
        return jnp.where(ids < mirrors, mirror_row, hub_row)

    def join(self, rows, hubs):
        parts = []
        for peer in range(self.peers):
            start = peer * self.block
            parts += [rows[start : start + self.slots], hubs]
        return jnp.concatenate(parts, axis=0)


def block_of(shape, axis, block):
    index = iota(shape, axis).astype(F32)
    number = jnp.floor((index + 0.5) * (1.0 / block))
    return number, index - block * number


def choose(lay, block, count_ref, list_ref):
    _, col_rest = block_of((lay.slots, lay.peers * block), 1, block)
    spread = (col_rest == iota(col_rest.shape, 0).astype(F32)).astype(BF16)
    wanted = list_ref[...]
    high, low = (wanted >> 4).astype(BF16), (wanted & 15).astype(BF16)
    placed = 16.0 * dot(high, spread) + dot(low, spread)
    shape = (lay.peers, lay.peers * block)
    peer, col = iota(shape, 0), iota(shape, 1)
    count = jnp.zeros(shape, I32)
    for index in range(lay.peers):
        count = jnp.where(peer == index, count_ref[0, index], count)
    slot = col - peer * block
    live = (slot >= 0) & (slot < count)
    chosen = jnp.sum(jnp.where(live, placed + 1.0, 0.0), axis=0, keepdims=True) - 1.0
    return chosen.astype(I32)


def gather_body(lay, count_ref, list_ref, rows_ref, hubs_ref, out_ref):
    rows = rows_ref.shape[0]
    chosen = choose(lay, lay.block, count_ref, list_ref)
    select = (iota((rows, lay.rows), 0) == chosen).astype(BF16)
    picked = dot(select, rows_ref[...], TN)
    out_ref[...] = lay.join(picked, hubs_ref[...].astype(F32)).astype(BF16)


def count_body(lay, count_ref, list_ref, src_ref, dst_ref, mask_ref, *refs):
    low_ref, high_ref, rows_ref, near_ref, wide_ref, sum_ref = refs
    chunk = min(CHUNK, src_ref.shape[0])
    steps = src_ref.shape[0] // chunk
    ids = iota((lay.rows, chunk), 0)
    for step in range(steps):
        span = pl.ds(step * chunk, chunk)
        src = lay.place(src_ref[span].reshape(1, chunk))
        keep = mask_ref[span].reshape(1, chunk) > 0
        dst = jnp.where(keep, lay.place(dst_ref[span].reshape(1, chunk)), -1)
        part = dot((ids == dst).astype(BF16), (ids == src).astype(BF16), NT)
        if step == 0:
            sum_ref[...] = part
        else:
            sum_ref[...] += part
    high = jnp.floor(sum_ref[...] * (1.0 / 256.0))
    low = (sum_ref[...] - 256.0 * high).astype(BF16)
    high = high.astype(BF16)
    low_ref[...] = low
    high_ref[...] = high
    ones = jnp.ones((16, lay.rows), BF16)
    counts = (dot(ones, low, NT) + 256.0 * dot(ones, high, NT))[:1]
    rounded = counts.astype(BF16).astype(F32)
    shape = (lay.wide_rows, lay.rows)
    row_block, row_rest = block_of(shape, 0, lay.wide)
    col_block, _ = block_of(shape, 1, lay.block)
    same = row_block == col_block
    spread = jnp.where(same & (row_rest == lay.block), rounded, 0.0)
    spread += jnp.where(same & (row_rest == lay.block + 1), counts - rounded, 0.0)
    _, row_rest = block_of((lay.rows, rows_ref.shape[1]), 0, lay.block)
    fold = (row_rest == iota(row_rest.shape, 1).astype(F32)).astype(BF16)
    rows_ref[...] = dot(spread.astype(BF16), fold).astype(BF16)
    near_ref[...] = choose(lay, lay.block, count_ref, list_ref)
    wide_ref[...] = choose(lay, lay.wide, count_ref, list_ref)


def forward_body(lay, table_ref, w_ref, low_ref, high_ref, rows_ref, out_ref):
    hidden = silu(dot(table_ref[...], w_ref[...])).astype(BF16)
    partial = dot(low_ref[...], hidden) + 256.0 * dot(high_ref[...], hidden)
    rest = jnp.zeros((lay.wide - lay.block, partial.shape[1]), F32)
    parts = []
    for start in range(0, lay.rows, lay.block):
        parts += [partial[start : start + lay.block], rest]
    out_ref[...] = (jnp.concatenate(parts, axis=0) + rows_ref[...].astype(F32)).astype(BF16)


def slope_body(table_ref, w_ref, low_ref, high_ref, slope_ref, table_t_ref, counts_ref):
    slope_ref[...] = silu_grad(dot(table_ref[...], w_ref[...]))

    def turned(ref):
        size = ref.shape[1]
        same = (iota((size, size), 0) == iota((size, size), 1)).astype(BF16)
        return dot(same, ref[...], NT)

    table_t_ref[...] = turned(table_ref).astype(BF16)
    counts_ref[...] = jnp.concatenate([turned(low_ref), turned(high_ref)], axis=0).astype(BF16)


def hub_sum_body(lay, back_ref, out_ref):
    width = back_ref.shape[1]
    hidden = jnp.zeros((lay.hubs, width), F32)
    counts = jnp.zeros((lay.wide - lay.block, width), F32)
    for peer in range(lay.peers):
        start = peer * lay.wide
        part = back_ref[start + lay.slots : start + lay.wide, :].astype(F32)
        hidden += part[: lay.hubs]
        counts += part[lay.hubs :]
    count = counts[0:1] + counts[1:2]
    shape = (lay.hubs, width)
    own = iota(shape, 1) == iota(shape, 0) + lay.slots
    degree = jnp.sum(jnp.where(own, count, 0.0), axis=1, keepdims=True)
    out_ref[:, :width] = hidden
    out_ref[:, width:] = jnp.broadcast_to(degree, (lay.hubs, out_ref.shape[1] - width))


def update_rows(states, cotangent, hidden_sum, degree, w_out, w_update):
    high, low = halves(hidden_sum)
    share = 1.0 / jnp.maximum(degree, 1.0)
    mixed = (states + (dot(high, w_out) + dot(low, w_out)) * share).astype(BF16)
    pre = dot(mixed, w_update)
    updated = (states + silu(pre)).astype(BF16)
    grad_pre = (cotangent * silu_grad(pre)).astype(BF16)
    grad_sum = (dot(grad_pre, w_update, NT) * share).astype(BF16)
    grad_hidden = dot(grad_sum, w_out, NT).astype(BF16)
    return updated, mixed, grad_pre, high, low, grad_sum, grad_hidden


def master_body(lay, n_far, near_ref, wide_ref, back_ref, *refs):
    far, refs = refs[:n_far], refs[n_far:]
    new_ref, mixed_ref, pre_ref, high_ref, low_ref, sum_ref, out_ref = refs[:7]
    near, sems = list(refs[-3:-1]) + list(refs[7:-3]), refs[-1]
    copies = [pltpu.make_async_copy(a, b, sems.at[i]) for i, (a, b) in enumerate(zip(far, near))]
    for copy in copies:
        copy.start()
    state_ref, cot_ref, w_out_ref, w_up_ref = near[:4]
    rows, width = state_ref.shape[0], back_ref.shape[1]
    select = (iota((rows, lay.wide_rows), 0) == wide_ref[...]).astype(BF16)
    back = back_ref[...]
    shape = (lay.wide_rows, lay.wide_rows)
    row_block, _ = block_of(shape, 0, lay.wide)
    taken = iota(shape, 1).astype(F32) == row_block * lay.wide + lay.block
    _, row_rest = block_of((lay.wide_rows, width), 0, lay.wide)
    own = row_rest == iota(row_rest.shape, 1).astype(F32)
    counts = jnp.where(own, dot(taken.astype(BF16), back), 0.0)
    degree = jnp.sum(dot(select, counts.astype(BF16)), axis=1, keepdims=True)
    hidden_sum = dot(select, back)
    for copy in copies:
        copy.wait()
    results = update_rows(
        state_ref[...].astype(F32),
        cot_ref[...].astype(F32),
        hidden_sum,
        degree,
        w_out_ref[...],
        w_up_ref[...],
    )
    updated, mixed, grad_pre, high, low, grad_sum, grad_hidden = results
    select = (iota((rows, lay.rows), 0) == near_ref[...]).astype(BF16)
    out_ref[...] = dot(select, grad_hidden, TN)
    new_ref[...] = updated
    mixed_ref[...] = mixed
    pre_ref[...] = grad_pre
    high_ref[...] = high
    low_ref[...] = low
    sum_ref[...] = grad_sum


def hub_body(
    lay,
    n_parts,
    *refs,
):
    parts = refs[:n_parts]
    state_ref, cot_ref, w_out_ref, w_up_ref, rows_ref = refs[n_parts : n_parts + 5]
    new_ref, mixed_ref, pre_ref, high_ref, low_ref, sum_ref, out_ref = refs[n_parts + 5 :]
    total = parts[0][...]
    for part in parts[1:]:
        total += part[...]
    width = rows_ref.shape[1]
    results = update_rows(
        state_ref[...].astype(F32),
        cot_ref[...].astype(F32),
        total[:, :width],
        total[:, width : width + 1],
        w_out_ref[...],
        w_up_ref[...],
    )
    updated, mixed, grad_pre, high, low, grad_sum, grad_hidden = results
    new_ref[...] = updated
    mixed_ref[...] = mixed
    pre_ref[...] = grad_pre
    high_ref[...] = high
    low_ref[...] = low
    sum_ref[...] = grad_sum
    out_ref[...] = lay.join(rows_ref[...], grad_hidden.astype(F32)).astype(BF16)


def weight_body(
    place_ref,
    mixed_ref,
    pre_ref,
    high_ref,
    low_ref,
    sum_ref,
    hub_mixed_ref,
    hub_pre_ref,
    hub_high_ref,
    hub_low_ref,
    hub_sum_ref,
    *outs,
):
    work = outs[-1]
    weight = place_ref[0].astype(F32)
    rows = mixed_ref.shape[1]
    grad_sum, hub_grad = sum_ref[...], hub_sum_ref[...]
    work[:rows, :] = dot(mixed_ref[...], pre_ref[...], TN) + weight * dot(
        hub_mixed_ref[...], hub_pre_ref[...], TN
    )
    hub_part = dot(hub_high_ref[...], hub_grad, TN) + dot(hub_low_ref[...], hub_grad, TN)
    main = dot(high_ref[...], grad_sum, TN) + dot(low_ref[...], grad_sum, TN)
    work[rows:, :] = main + weight * hub_part
    deal(work, place_ref[1], outs[:-1], len(outs) - 2)


def deal(work, place, outs, pieces=1):
    depth = outs[0].shape[0]
    start = pl.multiple_of(place * depth, depth)
    outs[0][...] = work[pl.ds(start, depth), :]
    piece = depth // pieces
    for index, out in enumerate(outs[1:]):
        start = (place ^ (index // pieces + 1)) * depth + (index % pieces) * piece
        out[...] = work[pl.ds(pl.multiple_of(start, piece), piece), :].astype(out.dtype)


def added(own_ref, terms):
    value = own_ref[...]
    for term in terms:
        value += term[...].astype(F32)
    return value


def share_body(size, apart, place_ref, *refs):
    ins, outs, works = refs[: -2 - size], refs[-2 - size : -2], refs[-2:]
    if apart:
        works[0][...] = added(ins[0], ins[1:2])
        works[1][...] = added(ins[2], ins[3:])
    else:
        value, split = added(ins[0], ins[1:]), works[0].shape[0]
        works[0][...] = value[:split]
        works[1][...] = value[split:]
    depths = [work.shape[0] // size for work in works]
    for step, out in enumerate(outs):
        parts = []
        for work, depth in zip(works, depths):
            start = pl.multiple_of((place_ref[0] ^ step) * depth, depth)
            parts.append(work[pl.ds(start, depth), :])
        out[...] = jnp.concatenate(parts, axis=0).astype(out.dtype)


def settle_body(own_ref, *refs):
    refs[-1][...] = added(own_ref, refs[:-1]).astype(BF16)


def finish_body(blocks, place_ref, own_ref, other_ref, update_ref, out_ref, in_ref):
    first = place_ref[0] == 0
    own, other = own_ref[...].astype(F32), other_ref[...].astype(F32)
    rows, hid = update_ref.shape[0], in_ref.shape[1]
    depth = own.shape[0] // blocks
    side = in_ref.shape[0] // (4 * blocks)
    split = depth - side
    for half in range(2):
        value = jnp.where(first, own, other) if half == 0 else jnp.where(first, other, own)
        for index in range(blocks):
            part = value[index * depth : (index + 1) * depth]
            start = (half * blocks + index) * split
            cut = min(max(rows - start, 0), split)
            if cut > 0:
                update_ref[start : start + cut, :] = part[:cut]
            if cut < split:
                out_ref[start + cut - rows : start + split - rows, :] = part[cut:split]
            start = (half * blocks + index) * side
            in_ref[start : start + side, :] = part[split:, :hid]
            start += in_ref.shape[0] // 2
            in_ref[start : start + side, :] = part[split:, hid:]


def backward_body(
    place_ref, grad_ref, far_counts_ref, far_slope_ref, far_table_ref, *refs
):
    far, near, sems = (far_counts_ref, far_slope_ref, far_table_ref), refs[-4:-1], refs[-1]
    copies = [pltpu.make_async_copy(a, b, sems.at[i]) for i, (a, b) in enumerate(zip(far, near))]
    for copy in copies:
        copy.start()
    counts_ref, slope_ref, table_t_ref = near
    grad = grad_ref[...]
    rows, work, refs = grad.shape[0], refs[-5], refs[:-5]
    copies[0].wait()
    both = dot(counts_ref[...], grad)
    copies[1].wait()
    high, low = halves((both[:rows] + 256.0 * both[rows:]) * slope_ref[...])
    copies[2].wait()
    table_t = table_t_ref[...]
    value = dot(table_t, high) + dot(table_t, low)
    half, hid = value.shape[0] // 2, value.shape[1]
    work[:, :hid] = value[:half]
    work[:, hid:] = value[half:]
    deal(work, place_ref[0], refs, len(refs) - 1)


def call(body, outs, args, scratch=(), flops=0, smem=0, limit=24, far=0):
    args = list(args)
    for index in range(len(args) - far, len(args)):
        args[index] = pltpu.with_memory_space_constraint(args[index], pltpu.HBM)
    outs = [jax.ShapeDtypeStruct(shape, kind) for shape, kind in outs]
    moved = sum(a.size * a.dtype.itemsize for a in list(args) + outs)
    vmem = pl.BlockSpec(memory_space=pltpu.VMEM)
    specs = [pl.BlockSpec(memory_space=pltpu.SMEM)] * smem + [vmem] * (len(args) - smem - far)
    specs += [pl.BlockSpec(memory_space=pl.ANY)] * far
    single = len(outs) == 1
    params = pltpu.CompilerParams(vmem_limit_bytes=limit << 20) if limit else None
    return pl.pallas_call(
        body,
        out_shape=outs[0] if single else outs,
        in_specs=specs,
        out_specs=vmem if single else [vmem] * len(outs),
        scratch_shapes=list(scratch),
        compiler_params=params,
        cost_estimate=pl.CostEstimate(
            flops=int(flops), bytes_accessed=int(moved), transcendentals=0
        ),
    )(*args)


PIECES = 1


class Cube:
    def __init__(self, n_group, n_dev, parts):
        self.total = n_group * n_dev
        self.size, self.steps, self.place = 1, [0], 0
        for axis, stride, size in parts:
            unit = stride * (n_dev if axis == "group" else 1)
            place = lax.rem(lax.div(lax.axis_index(axis), stride), size)
            self.place = self.place * size + place
            self.steps = [s | (i * unit) for s in self.steps for i in range(size)]
            self.size *= size

    def send(self, value, step):
        pairs = [(i, i ^ self.steps[step]) for i in range(self.total)]
        return lax.ppermute(value, ("group", "dev"), pairs)

    def scatter(self, value):
        blocks = value.reshape(self.size, -1, value.shape[1])
        own = lax.dynamic_index_in_dim(blocks, self.place, 0, False)
        terms = []
        for step in range(1, self.size):
            block = lax.dynamic_index_in_dim(blocks, self.place ^ step, 0, False)
            terms.append(self.send(block.astype(BF16), step))
        return own, terms

    def gather(self, value):
        parts = [value] + [self.send(value, step) for step in range(1, self.size)]
        bit = 1
        while bit < self.size:
            flip = (self.place & bit) > 0
            parts = [jnp.where(flip, parts[i ^ bit], parts[i]) for i in range(self.size)]
            bit *= 2
        return jnp.concatenate(parts, axis=0)


def total(own, terms):
    for term in terms:
        own += term.astype(F32)
    return own


def share(cube, depths, ins):
    apart = isinstance(ins[0], list)
    flat_ins = ins[0] + ins[1] if apart else ins
    width = flat_ins[0].shape[1]
    rows = [depth // cube.size for depth in depths]
    if any(count % 8 for count in rows):
        if apart:
            values = [total(group[0], group[1:]) for group in ins]
        else:
            values = jnp.split(total(ins[0], ins[1:]), [depths[0]], axis=0)
        values = [value.reshape(cube.size, -1, width) for value in values]
        return cube.scatter(jnp.concatenate(values, axis=1).reshape(-1, width))
    shape = (sum(rows), width)
    own, *sent = call(
        functools.partial(share_body, cube.size, apart),
        [(shape, F32)] + [(shape, BF16)] * (cube.size - 1),
        [cube.place.reshape(1), *flat_ins],
        scratch=[pltpu.VMEM((depth, width), F32) for depth in depths],
        smem=1,
    )
    return own, [cube.send(block, step + 1) for step, block in enumerate(sent)]


def shards(
    node_state,
    hub_state,
    w_edge_in,
    w_edge_out,
    w_update,
    edge_src,
    edge_dst,
    edge_mask,
    send_list,
    send_count,
    node_cot,
    hub_cot,
    *,
    n_group,
    n_dev,
):
    rows, width = node_state.shape
    hid = w_edge_in.shape[1]
    slots = send_list.shape[2]
    hubs = hub_state.shape[0]
    lay = Layout(n_dev, slots, hubs)
    both = ("group", "dev")
    run = functools.partial(call, limit=24 if lay.rows <= 512 else 48)
    def body(function, *static):
        return functools.partial(function, *static)

    packed = run(
        body(gather_body, lay),
        [((lay.rows, width), BF16)],
        [send_count, send_list[0], node_state, hub_state],
        smem=1,
        limit=None,
    )
    table = lax.all_to_all(packed, "dev", 0, 0, tiled=True)

    square = ((lay.rows, lay.rows), BF16)
    edges = [edge_src, edge_dst, edge_mask]
    low, high, count_rows, near, wide = run(
        body(count_body, lay),
        [
            square,
            square,
            ((lay.wide_rows, hid), BF16),
            ((1, lay.rows), I32),
            ((1, lay.wide_rows), I32),
        ],
        [send_count, send_list[0]] + edges,
        scratch=[pltpu.VMEM((lay.rows, lay.rows), F32)],
        flops=2 * edge_src.shape[0] * lay.rows * lay.rows,
        smem=1,
    )
    message = run(
        body(forward_body, lay),
        [((lay.wide_rows, hid), BF16)],
        [table, w_edge_in, low, high, count_rows],
    )
    back = lax.all_to_all(message, "dev", 0, 0, tiled=True)
    turned = run(
        slope_body,
        [((lay.rows, hid), F32), ((width, lay.rows), BF16), ((2 * lay.rows, lay.rows), BF16)],
        [table, w_edge_in, low, high],
        flops=2 * lay.rows * width * hid,
    )
    back, (slope, table_t, counts_t) = lax.optimization_barrier((back, turned))

    hub_part = run(body(hub_sum_body, lay), [((hubs, hid + 128), F32)], [back])
    group_cube = Cube(n_group, n_dev, [("group", 1, n_group)])
    parts = [hub_part] + [group_cube.send(hub_part, step) for step in range(1, n_group)]

    def row_outs(count):
        return [
            ((count, width), BF16),
            ((count, width), BF16),
            ((count, width), BF16),
            ((count, hid), BF16),
            ((count, hid), BF16),
            ((count, width), BF16),
        ]

    far = [node_state, node_cot, w_edge_out, w_update, hub_state, hub_cot]
    master = run(
        body(master_body, lay, len(far)),
        row_outs(rows) + [((lay.rows, hid), F32)] + [(a.shape, a.dtype) for a in far[2:]],
        [near, wide, back] + far,
        scratch=[
            pltpu.VMEM((rows, width), BF16),
            pltpu.VMEM((rows, width), BF16),
            pltpu.SemaphoreType.DMA((len(far),)),
        ],
        flops=2 * rows * (2 * lay.rows * hid + 2 * width * width + 2 * width * hid),
        far=len(far),
    )
    new_state, saved, grad_rows = master[0], list(master[1:6]), master[6]
    w_out, w_up, hub_rows, hub_grads = master[7:]
    new_hub, *hub_saved, grad_message = run(
        body(hub_body, lay, n_group),
        row_outs(hubs) + [((lay.rows, hid), BF16)],
        parts + [hub_rows, hub_grads, w_out, w_up, grad_rows],
    )
    grad_table = lax.all_to_all(grad_message, "dev", 0, 0, tiled=True)

    core = Cube(n_group, n_dev, [("group", 1, 2)])
    flat = Cube(n_group, n_dev, [("group", 2, n_group // 2), ("dev", 1, 2)])
    line = Cube(n_group, n_dev, [("dev", 2, n_dev // 2)])
    upper_rows = width + hid

    half, quarter = upper_rows // 2, width // 4
    first = (lax.axis_index("group") == 0).astype(I32)
    own, *sent = run(
        weight_body,
        [((half, width), F32)] + [((half // PIECES, width), BF16)] * PIECES,
        [jnp.stack([first, core.place])] + saved + hub_saved,
        scratch=[pltpu.VMEM((upper_rows, width), F32)],
        flops=2 * rows * width * (width + 2 * hid),
        smem=1,
    )
    upper = [own] + [core.send(block, 1) for block in sent]
    side, *sent = run(
        backward_body,
        [((quarter, width), F32)] + [((quarter // PIECES, width), BF16)] * PIECES,
        [core.place.reshape(1), grad_table, counts_t, slope, table_t],
        scratch=[
            pltpu.VMEM((width // 2, width), F32),
            pltpu.VMEM(counts_t.shape, BF16),
            pltpu.VMEM(slope.shape, F32),
            pltpu.VMEM(table_t.shape, BF16),
            pltpu.SemaphoreType.DMA((3,)),
        ],
        far=3,
        flops=2 * lay.rows * hid * (lay.rows + width) * 2,
        smem=1,
    )
    side = [side] + [core.send(block, 1) for block in sent]
    depths = [half, quarter]
    for cube in (flat, line):
        own, terms = share(cube, depths, [upper, side] if cube is flat else [own, *terms])
        depths = [depth // cube.size for depth in depths]
    block = sum(depths)
    if depths[1] % 8 == 0:
        whole = run(settle_body, [((block, width), BF16)], [own, *terms])
    else:
        whole = total(own, terms).astype(BF16)
    for cube in (line, flat):
        whole = cube.gather(whole)
    if depths[1] % 8 == 0:
        grad_update, grad_out, grad_in = run(
            body(finish_body, n_group * n_dev // 2),
            [((width, width), F32), ((hid, width), F32), ((width, hid), F32)],
            [core.place.reshape(1), whole, core.send(whole, 1)],
            smem=1,
        )
        return new_state, new_hub, grad_in, grad_out, grad_update
    whole = core.gather(whole).reshape(n_group * n_dev, -1, width).astype(F32)
    upper = whole[:, : depths[0]].reshape(-1, width)
    side = whole[:, depths[0] :].reshape(-1, width)
    side = jnp.concatenate([side[:, :hid], side[:, hid:]], axis=0)
    return new_state, new_hub, side, upper[width:], upper[:width]


def solution(mesh):
    def body(*args):
        return shards(*args, n_group=mesh.shape["group"], n_dev=mesh.shape["dev"])

    return jax.shard_map(
        body,
        mesh=mesh,
        in_specs=(
            P(("group", "dev"), None),
            P("dev", None),
            P(),
            P(),
            P(),
            P(("group", "dev")),
            P(("group", "dev")),
            P(("group", "dev")),
            P(("group", "dev"), None, None),
            P(("group", "dev"), None),
            P(("group", "dev"), None),
            P("dev", None),
        ),
        out_specs=(P(("group", "dev"), None), P("dev", None), P(), P(), P()),
        check_vma=False,
    )
```

```python
import functools

import jax
import jax.numpy as jnp
from jax import lax
from jax.experimental import pallas as pl
from jax.experimental.pallas import tpu as pltpu
from jax.sharding import PartitionSpec as P

F32 = jnp.float32
BF16 = jnp.bfloat16
I32 = jnp.int32
CHUNK = 512
NN = ((1,), (0,))
NT = ((1,), (1,))
TN = ((0,), (0,))


def dot(left, right, dims=NN):
    return lax.dot_general(left, right, (dims, ((), ())), preferred_element_type=F32)


def halves(value):
    high = value.astype(BF16)
    return high, (value - high.astype(F32)).astype(BF16)


def silu(values):
    return values * jax.nn.sigmoid(values)


def silu_grad(values):
    sigmoid_v = jax.nn.sigmoid(values)
    return sigmoid_v * (1.0 + values * (1.0 - sigmoid_v))


def iota(shape, axis):
    return lax.broadcasted_iota(I32, shape, axis)


class Layout:
    def __init__(self, peers, slots, hubs):
        self.peers, self.slots, self.hubs = peers, slots, hubs
        self.block = slots + hubs
        self.wide = -(-(self.block + 2) // 16) * 16
        self.rows, self.wide_rows = peers * self.block, peers * self.wide

    def place(self, ids):
        mirrors = self.peers * self.slots
        slot_bits, hub_bits = self.slots.bit_length() - 1, self.hubs.bit_length() - 1
        hub_ids = ids - mirrors
        mirror_row = (ids >> slot_bits) * self.block + (ids & (self.slots - 1))
        hub_row = (hub_ids >> hub_bits) * self.block + self.slots + (hub_ids & (self.hubs - 1))
        return jnp.where(ids < mirrors, mirror_row, hub_row)

    def join(self, rows, hubs):
        parts = []
        for peer in range(self.peers):
            start = peer * self.block
            parts += [rows[start : start + self.slots], hubs]
        return jnp.concatenate(parts, axis=0)


def block_of(shape, axis, block):
    index = iota(shape, axis).astype(F32)
    number = jnp.floor((index + 0.5) * (1.0 / block))
    return number, index - block * number


def choose(lay, block, count_ref, list_ref):
    _, col_rest = block_of((lay.slots, lay.peers * block), 1, block)
    spread = (col_rest == iota(col_rest.shape, 0).astype(F32)).astype(BF16)
    wanted = list_ref[...]
    high, low = (wanted >> 4).astype(BF16), (wanted & 15).astype(BF16)
    placed = 16.0 * dot(high, spread) + dot(low, spread)
    shape = (lay.peers, lay.peers * block)
    peer, col = iota(shape, 0), iota(shape, 1)
    count = jnp.zeros(shape, I32)
    for index in range(lay.peers):
        count = jnp.where(peer == index, count_ref[0, index], count)
    slot = col - peer * block
    live = (slot >= 0) & (slot < count)
    chosen = jnp.sum(jnp.where(live, placed + 1.0, 0.0), axis=0, keepdims=True) - 1.0
    return chosen.astype(I32)


def gather_body(lay, count_ref, list_ref, rows_ref, hubs_ref, out_ref):
    rows = rows_ref.shape[0]
    chosen = choose(lay, lay.block, count_ref, list_ref)
    select = (iota((rows, lay.rows), 0) == chosen).astype(BF16)
    picked = dot(select, rows_ref[...], TN)
    out_ref[...] = lay.join(picked, hubs_ref[...].astype(F32)).astype(BF16)


def count_body(lay, count_ref, list_ref, src_ref, dst_ref, mask_ref, *refs):
    low_ref, high_ref, rows_ref, near_ref, wide_ref, sum_ref = refs
    chunk = min(CHUNK, src_ref.shape[0])
    steps = src_ref.shape[0] // chunk
    ids = iota((lay.rows, chunk), 0)
    for step in range(steps):
        span = pl.ds(step * chunk, chunk)
        src = lay.place(src_ref[span].reshape(1, chunk))
        keep = mask_ref[span].reshape(1, chunk) > 0
        dst = jnp.where(keep, lay.place(dst_ref[span].reshape(1, chunk)), -1)
        part = dot((ids == dst).astype(BF16), (ids == src).astype(BF16), NT)
        if step == 0:
            sum_ref[...] = part
        else:
            sum_ref[...] += part
    high = jnp.floor(sum_ref[...] * (1.0 / 256.0))
    low = (sum_ref[...] - 256.0 * high).astype(BF16)
    high = high.astype(BF16)
    low_ref[...] = low
    high_ref[...] = high
    ones = jnp.ones((16, lay.rows), BF16)
    counts = (dot(ones, low, NT) + 256.0 * dot(ones, high, NT))[:1]
    rounded = counts.astype(BF16).astype(F32)
    shape = (lay.wide_rows, lay.rows)
    row_block, row_rest = block_of(shape, 0, lay.wide)
    col_block, _ = block_of(shape, 1, lay.block)
    same = row_block == col_block
    spread = jnp.where(same & (row_rest == lay.block), rounded, 0.0)
    spread += jnp.where(same & (row_rest == lay.block + 1), counts - rounded, 0.0)
    _, row_rest = block_of((lay.rows, rows_ref.shape[1]), 0, lay.block)
    fold = (row_rest == iota(row_rest.shape, 1).astype(F32)).astype(BF16)
    rows_ref[...] = dot(spread.astype(BF16), fold).astype(BF16)
    near_ref[...] = choose(lay, lay.block, count_ref, list_ref)
    wide_ref[...] = choose(lay, lay.wide, count_ref, list_ref)


def forward_body(lay, table_ref, w_ref, low_ref, high_ref, rows_ref, out_ref):
    hidden = silu(dot(table_ref[...], w_ref[...])).astype(BF16)
    partial = dot(low_ref[...], hidden) + 256.0 * dot(high_ref[...], hidden)
    rest = jnp.zeros((lay.wide - lay.block, partial.shape[1]), F32)
    parts = []
    for start in range(0, lay.rows, lay.block):
        parts += [partial[start : start + lay.block], rest]
    out_ref[...] = (jnp.concatenate(parts, axis=0) + rows_ref[...].astype(F32)).astype(BF16)


def slope_body(table_ref, w_ref, low_ref, high_ref, slope_ref, table_t_ref, counts_ref):
    slope_ref[...] = silu_grad(dot(table_ref[...], w_ref[...]))

    def turned(ref):
        size = ref.shape[1]
        same = (iota((size, size), 0) == iota((size, size), 1)).astype(BF16)
        return dot(same, ref[...], NT)

    table_t_ref[...] = turned(table_ref).astype(BF16)
    counts_ref[...] = jnp.concatenate([turned(low_ref), turned(high_ref)], axis=0).astype(BF16)


def hub_sum_body(lay, back_ref, out_ref):
    width = back_ref.shape[1]
    hidden = jnp.zeros((lay.hubs, width), F32)
    counts = jnp.zeros((lay.wide - lay.block, width), F32)
    for peer in range(lay.peers):
        start = peer * lay.wide
        part = back_ref[start + lay.slots : start + lay.wide, :].astype(F32)
        hidden += part[: lay.hubs]
        counts += part[lay.hubs :]
    count = counts[0:1] + counts[1:2]
    shape = (lay.hubs, width)
    own = iota(shape, 1) == iota(shape, 0) + lay.slots
    degree = jnp.sum(jnp.where(own, count, 0.0), axis=1, keepdims=True)
    out_ref[:, :width] = hidden
    out_ref[:, width:] = jnp.broadcast_to(degree, (lay.hubs, out_ref.shape[1] - width))


def update_rows(states, cotangent, hidden_sum, degree, w_out, w_update):
    high, low = halves(hidden_sum)
    share = 1.0 / jnp.maximum(degree, 1.0)
    mixed = (states + (dot(high, w_out) + dot(low, w_out)) * share).astype(BF16)
    pre = dot(mixed, w_update)
    grad_pre = (cotangent * silu_grad(pre)).astype(BF16)
    grad_sum = (dot(grad_pre, w_update, NT) * share).astype(BF16)
    grad_hidden = dot(grad_sum, w_out, NT).astype(BF16)
    return mixed, pre, grad_pre, high, low, grad_sum, grad_hidden


def state_body(mixed_ref, w_up_ref, far_ref, new_ref, state_ref, sem):
    copy = pltpu.make_async_copy(far_ref, state_ref, sem)
    copy.start()
    change = silu(dot(mixed_ref[...], w_up_ref[...]))
    copy.wait()
    new_ref[...] = (state_ref[...].astype(F32) + change).astype(BF16)


def master_body(lay, n_far, near_ref, wide_ref, back_ref, *refs):
    far, refs = refs[:n_far], refs[n_far:]
    mixed_ref, pre_ref, high_ref, low_ref, sum_ref, out_ref = refs[:6]
    near, sems = list(refs[-3:-1]) + list(refs[6:-3]), refs[-1]
    copies = [pltpu.make_async_copy(a, b, sems.at[i]) for i, (a, b) in enumerate(zip(far, near))]
    for copy in copies:
        copy.start()
    state_ref, cot_ref, w_out_ref, w_up_ref = near[:4]
    rows, width = state_ref.shape[0], back_ref.shape[1]
    select = (iota((rows, lay.wide_rows), 0) == wide_ref[...]).astype(BF16)
    back = back_ref[...]
    shape = (lay.wide_rows, lay.wide_rows)
    row_block, _ = block_of(shape, 0, lay.wide)
    taken = iota(shape, 1).astype(F32) == row_block * lay.wide + lay.block
    _, row_rest = block_of((lay.wide_rows, width), 0, lay.wide)
    own = row_rest == iota(row_rest.shape, 1).astype(F32)
    counts = jnp.where(own, dot(taken.astype(BF16), back), 0.0)
    degree = jnp.sum(dot(select, counts.astype(BF16)), axis=1, keepdims=True)
    hidden_sum = dot(select, back)
    for copy in copies:
        copy.wait()
    results = update_rows(
        state_ref[...].astype(F32),
        cot_ref[...].astype(F32),
        hidden_sum,
        degree,
        w_out_ref[...],
        w_up_ref[...],
    )
    mixed, _, grad_pre, high, low, grad_sum, grad_hidden = results
    select = (iota((rows, lay.rows), 0) == near_ref[...]).astype(BF16)
    out_ref[...] = dot(select, grad_hidden, TN)
    mixed_ref[...] = mixed
    pre_ref[...] = grad_pre
    high_ref[...] = high
    low_ref[...] = low
    sum_ref[...] = grad_sum


def hub_body(
    lay,
    n_parts,
    *refs,
):
    parts = refs[:n_parts]
    state_ref, cot_ref, w_out_ref, w_up_ref, rows_ref = refs[n_parts : n_parts + 5]
    new_ref, mixed_ref, pre_ref, high_ref, low_ref, sum_ref, out_ref = refs[n_parts + 5 :]
    total = parts[0][...]
    for part in parts[1:]:
        total += part[...]
    width = rows_ref.shape[1]
    states = state_ref[...].astype(F32)
    results = update_rows(
        states,
        cot_ref[...].astype(F32),
        total[:, :width],
        total[:, width : width + 1],
        w_out_ref[...],
        w_up_ref[...],
    )
    mixed, pre, grad_pre, high, low, grad_sum, grad_hidden = results
    new_ref[...] = (states + silu(pre)).astype(BF16)
    mixed_ref[...] = mixed
    pre_ref[...] = grad_pre
    high_ref[...] = high
    low_ref[...] = low
    sum_ref[...] = grad_sum
    out_ref[...] = lay.join(rows_ref[...], grad_hidden.astype(F32)).astype(BF16)


def weight_body(
    place_ref,
    mixed_ref,
    pre_ref,
    high_ref,
    low_ref,
    sum_ref,
    hub_mixed_ref,
    hub_pre_ref,
    hub_high_ref,
    hub_low_ref,
    hub_sum_ref,
    *outs,
):
    work = outs[-1]
    weight = place_ref[0].astype(F32)
    rows = mixed_ref.shape[1]
    grad_sum, hub_grad = sum_ref[...], hub_sum_ref[...]
    work[:rows, :] = dot(mixed_ref[...], pre_ref[...], TN) + weight * dot(
        hub_mixed_ref[...], hub_pre_ref[...], TN
    )
    hub_part = dot(hub_high_ref[...], hub_grad, TN) + dot(hub_low_ref[...], hub_grad, TN)
    main = dot(high_ref[...], grad_sum, TN) + dot(low_ref[...], grad_sum, TN)
    work[rows:, :] = main + weight * hub_part
    deal(work, place_ref[1], outs[:-1], len(outs) - 2)


def deal(work, place, outs, pieces=1):
    depth = outs[0].shape[0]
    start = pl.multiple_of(place * depth, depth)
    outs[0][...] = work[pl.ds(start, depth), :]
    piece = depth // pieces
    for index, out in enumerate(outs[1:]):
        start = (place ^ (index // pieces + 1)) * depth + (index % pieces) * piece
        out[...] = work[pl.ds(pl.multiple_of(start, piece), piece), :].astype(out.dtype)


def added(own_ref, terms):
    value = own_ref[...]
    for term in terms:
        value += term[...].astype(F32)
    return value


def share_body(size, apart, place_ref, *refs):
    ins, outs, works = refs[: -2 - size], refs[-2 - size : -2], refs[-2:]
    if apart:
        works[0][...] = added(ins[0], ins[1:2])
        works[1][...] = added(ins[2], ins[3:])
    else:
        value, split = added(ins[0], ins[1:]), works[0].shape[0]
        works[0][...] = value[:split]
        works[1][...] = value[split:]
    depths = [work.shape[0] // size for work in works]
    for step, out in enumerate(outs):
        parts = []
        for work, depth in zip(works, depths):
            start = pl.multiple_of((place_ref[0] ^ step) * depth, depth)
            parts.append(work[pl.ds(start, depth), :])
        out[...] = jnp.concatenate(parts, axis=0).astype(out.dtype)


def settle_body(own_ref, *refs):
    refs[-1][...] = added(own_ref, refs[:-1]).astype(BF16)


def finish_body(blocks, place_ref, own_ref, other_ref, update_ref, out_ref, in_ref):
    first = place_ref[0] == 0
    own, other = own_ref[...].astype(F32), other_ref[...].astype(F32)
    rows, hid = update_ref.shape[0], in_ref.shape[1]
    depth = own.shape[0] // blocks
    side = in_ref.shape[0] // (4 * blocks)
    split = depth - side
    for half in range(2):
        value = jnp.where(first, own, other) if half == 0 else jnp.where(first, other, own)
        for index in range(blocks):
            part = value[index * depth : (index + 1) * depth]
            start = (half * blocks + index) * split
            cut = min(max(rows - start, 0), split)
            if cut > 0:
                update_ref[start : start + cut, :] = part[:cut]
            if cut < split:
                out_ref[start + cut - rows : start + split - rows, :] = part[cut:split]
            start = (half * blocks + index) * side
            in_ref[start : start + side, :] = part[split:, :hid]
            start += in_ref.shape[0] // 2
            in_ref[start : start + side, :] = part[split:, hid:]


def backward_body(
    place_ref, grad_ref, far_counts_ref, far_slope_ref, far_table_ref, *refs
):
    far, near, sems = (far_counts_ref, far_slope_ref, far_table_ref), refs[-4:-1], refs[-1]
    copies = [pltpu.make_async_copy(a, b, sems.at[i]) for i, (a, b) in enumerate(zip(far, near))]
    for copy in copies:
        copy.start()
    counts_ref, slope_ref, table_t_ref = near
    grad = grad_ref[...]
    rows, work, refs = grad.shape[0], refs[-5], refs[:-5]
    copies[0].wait()
    both = dot(counts_ref[...], grad)
    copies[1].wait()
    high, low = halves((both[:rows] + 256.0 * both[rows:]) * slope_ref[...])
    copies[2].wait()
    table_t = table_t_ref[...]
    value = dot(table_t, high) + dot(table_t, low)
    half, hid = value.shape[0] // 2, value.shape[1]
    work[:, :hid] = value[:half]
    work[:, hid:] = value[half:]
    deal(work, place_ref[0], refs, len(refs) - 1)


def call(body, outs, args, scratch=(), flops=0, smem=0, limit=24, far=0):
    args = list(args)
    for index in range(len(args) - far, len(args)):
        args[index] = pltpu.with_memory_space_constraint(args[index], pltpu.HBM)
    outs = [jax.ShapeDtypeStruct(shape, kind) for shape, kind in outs]
    moved = sum(a.size * a.dtype.itemsize for a in list(args) + outs)
    vmem = pl.BlockSpec(memory_space=pltpu.VMEM)
    specs = [pl.BlockSpec(memory_space=pltpu.SMEM)] * smem + [vmem] * (len(args) - smem - far)
    specs += [pl.BlockSpec(memory_space=pl.ANY)] * far
    single = len(outs) == 1
    params = pltpu.CompilerParams(vmem_limit_bytes=limit << 20) if limit else None
    return pl.pallas_call(
        body,
        out_shape=outs[0] if single else outs,
        in_specs=specs,
        out_specs=vmem if single else [vmem] * len(outs),
        scratch_shapes=list(scratch),
        compiler_params=params,
        cost_estimate=pl.CostEstimate(
            flops=int(flops), bytes_accessed=int(moved), transcendentals=0
        ),
    )(*args)


PIECES = 1


class Cube:
    def __init__(self, n_group, n_dev, parts):
        self.total = n_group * n_dev
        self.size, self.steps, self.place = 1, [0], 0
        for axis, stride, size in parts:
            unit = stride * (n_dev if axis == "group" else 1)
            place = lax.rem(lax.div(lax.axis_index(axis), stride), size)
            self.place = self.place * size + place
            self.steps = [s | (i * unit) for s in self.steps for i in range(size)]
            self.size *= size

    def send(self, value, step):
        pairs = [(i, i ^ self.steps[step]) for i in range(self.total)]
        return lax.ppermute(value, ("group", "dev"), pairs)

    def scatter(self, value):
        blocks = value.reshape(self.size, -1, value.shape[1])
        own = lax.dynamic_index_in_dim(blocks, self.place, 0, False)
        terms = []
        for step in range(1, self.size):
            block = lax.dynamic_index_in_dim(blocks, self.place ^ step, 0, False)
            terms.append(self.send(block.astype(BF16), step))
        return own, terms

    def gather(self, value):
        parts = [value] + [self.send(value, step) for step in range(1, self.size)]
        bit = 1
        while bit < self.size:
            flip = (self.place & bit) > 0
            parts = [jnp.where(flip, parts[i ^ bit], parts[i]) for i in range(self.size)]
            bit *= 2
        return jnp.concatenate(parts, axis=0)


def total(own, terms):
    for term in terms:
        own += term.astype(F32)
    return own


def share(cube, depths, ins):
    apart = isinstance(ins[0], list)
    flat_ins = ins[0] + ins[1] if apart else ins
    width = flat_ins[0].shape[1]
    rows = [depth // cube.size for depth in depths]
    if any(count % 8 for count in rows):
        if apart:
            values = [total(group[0], group[1:]) for group in ins]
        else:
            values = jnp.split(total(ins[0], ins[1:]), [depths[0]], axis=0)
        values = [value.reshape(cube.size, -1, width) for value in values]
        return cube.scatter(jnp.concatenate(values, axis=1).reshape(-1, width))
    shape = (sum(rows), width)
    own, *sent = call(
        functools.partial(share_body, cube.size, apart),
        [(shape, F32)] + [(shape, BF16)] * (cube.size - 1),
        [cube.place.reshape(1), *flat_ins],
        scratch=[pltpu.VMEM((depth, width), F32) for depth in depths],
        smem=1,
    )
    return own, [cube.send(block, step + 1) for step, block in enumerate(sent)]


def shards(
    node_state,
    hub_state,
    w_edge_in,
    w_edge_out,
    w_update,
    edge_src,
    edge_dst,
    edge_mask,
    send_list,
    send_count,
    node_cot,
    hub_cot,
    *,
    n_group,
    n_dev,
):
    rows, width = node_state.shape
    hid = w_edge_in.shape[1]
    slots = send_list.shape[2]
    hubs = hub_state.shape[0]
    lay = Layout(n_dev, slots, hubs)
    both = ("group", "dev")
    run = functools.partial(call, limit=24 if lay.rows <= 512 else 48)
    def body(function, *static):
        return functools.partial(function, *static)

    packed = run(
        body(gather_body, lay),
        [((lay.rows, width), BF16)],
        [send_count, send_list[0], node_state, hub_state],
        smem=1,
        limit=None,
    )
    table = lax.all_to_all(packed, "dev", 0, 0, tiled=True)

    square = ((lay.rows, lay.rows), BF16)
    edges = [edge_src, edge_dst, edge_mask]
    low, high, count_rows, near, wide = run(
        body(count_body, lay),
        [
            square,
            square,
            ((lay.wide_rows, hid), BF16),
            ((1, lay.rows), I32),
            ((1, lay.wide_rows), I32),
        ],
        [send_count, send_list[0]] + edges,
        scratch=[pltpu.VMEM((lay.rows, lay.rows), F32)],
        flops=2 * edge_src.shape[0] * lay.rows * lay.rows,
        smem=1,
    )
    message = run(
        body(forward_body, lay),
        [((lay.wide_rows, hid), BF16)],
        [table, w_edge_in, low, high, count_rows],
    )
    back = lax.all_to_all(message, "dev", 0, 0, tiled=True)
    turned = run(
        slope_body,
        [((lay.rows, hid), F32), ((width, lay.rows), BF16), ((2 * lay.rows, lay.rows), BF16)],
        [table, w_edge_in, low, high],
        flops=2 * lay.rows * width * hid,
    )
    back, (slope, table_t, counts_t) = lax.optimization_barrier((back, turned))

    hub_part = run(body(hub_sum_body, lay), [((hubs, hid + 128), F32)], [back])
    group_cube = Cube(n_group, n_dev, [("group", 1, n_group)])
    parts = [hub_part] + [group_cube.send(hub_part, step) for step in range(1, n_group)]

    def row_outs(count):
        return [
            ((count, width), BF16),
            ((count, width), BF16),
            ((count, hid), BF16),
            ((count, hid), BF16),
            ((count, width), BF16),
        ]

    far = [node_state, node_cot, w_edge_out, w_update, hub_state, hub_cot]
    master = run(
        body(master_body, lay, len(far)),
        row_outs(rows) + [((lay.rows, hid), F32)] + [(a.shape, a.dtype) for a in far[2:]],
        [near, wide, back] + far,
        scratch=[
            pltpu.VMEM((rows, width), BF16),
            pltpu.VMEM((rows, width), BF16),
            pltpu.SemaphoreType.DMA((len(far),)),
        ],
        flops=2 * rows * (2 * lay.rows * hid + 2 * width * width + 2 * width * hid),
        far=len(far),
    )
    saved, grad_rows = list(master[:5]), master[5]
    w_out, w_up, hub_rows, hub_grads = master[6:]
    new_hub, *hub_saved, grad_message = run(
        body(hub_body, lay, n_group),
        [((hubs, width), BF16)] + row_outs(hubs) + [((lay.rows, hid), BF16)],
        parts + [hub_rows, hub_grads, w_out, w_up, grad_rows],
    )
    grad_table = lax.all_to_all(grad_message, "dev", 0, 0, tiled=True)

    core = Cube(n_group, n_dev, [("group", 1, 2)])
    flat = Cube(n_group, n_dev, [("group", 2, n_group // 2), ("dev", 1, 2)])
    line = Cube(n_group, n_dev, [("dev", 2, n_dev // 2)])
    upper_rows = width + hid

    half, quarter = upper_rows // 2, width // 4
    first = (lax.axis_index("group") == 0).astype(I32)
    own, *sent = run(
        weight_body,
        [((half, width), F32)] + [((half // PIECES, width), BF16)] * PIECES,
        [jnp.stack([first, core.place])] + saved + hub_saved,
        scratch=[pltpu.VMEM((upper_rows, width), F32)],
        flops=2 * rows * width * (width + 2 * hid),
        smem=1,
    )
    upper = [own] + [core.send(block, 1) for block in sent]
    side, *sent = run(
        backward_body,
        [((quarter, width), F32)] + [((quarter // PIECES, width), BF16)] * PIECES,
        [core.place.reshape(1), grad_table, counts_t, slope, table_t],
        scratch=[
            pltpu.VMEM((width // 2, width), F32),
            pltpu.VMEM(counts_t.shape, BF16),
            pltpu.VMEM(slope.shape, F32),
            pltpu.VMEM(table_t.shape, BF16),
            pltpu.SemaphoreType.DMA((3,)),
        ],
        far=3,
        flops=2 * lay.rows * hid * (lay.rows + width) * 2,
        smem=1,
    )
    side = [side] + [core.send(block, 1) for block in sent]
    depths = [half, quarter]
    for cube in (flat, line):
        own, terms = share(cube, depths, [upper, side] if cube is flat else [own, *terms])
        depths = [depth // cube.size for depth in depths]
    block = sum(depths)
    if depths[1] % 8 == 0:
        whole = run(settle_body, [((block, width), BF16)], [own, *terms])
    else:
        whole = total(own, terms).astype(BF16)
    new_state = run(
        state_body,
        [((rows, width), BF16)],
        [saved[0], w_up, node_state],
        scratch=[pltpu.VMEM((rows, width), BF16), pltpu.SemaphoreType.DMA],
        flops=2 * rows * width * width,
        far=1,
    )
    whole, new_state = lax.optimization_barrier((line.gather(whole), new_state))
    whole = flat.gather(whole)
    if depths[1] % 8 == 0:
        grad_update, grad_out, grad_in = run(
            body(finish_body, n_group * n_dev // 2),
            [((width, width), F32), ((hid, width), F32), ((width, hid), F32)],
            [core.place.reshape(1), whole, core.send(whole, 1)],
            smem=1,
        )
        return new_state, new_hub, grad_in, grad_out, grad_update
    whole = core.gather(whole).reshape(n_group * n_dev, -1, width).astype(F32)
    upper = whole[:, : depths[0]].reshape(-1, width)
    side = whole[:, depths[0] :].reshape(-1, width)
    side = jnp.concatenate([side[:, :hid], side[:, hid:]], axis=0)
    return new_state, new_hub, side, upper[width:], upper[:width]


def solution(mesh):
    def body(*args):
        return shards(*args, n_group=mesh.shape["group"], n_dev=mesh.shape["dev"])

    return jax.shard_map(
        body,
        mesh=mesh,
        in_specs=(
            P(("group", "dev"), None),
            P("dev", None),
            P(),
            P(),
            P(),
            P(("group", "dev")),
            P(("group", "dev")),
            P(("group", "dev")),
            P(("group", "dev"), None, None),
            P(("group", "dev"), None),
            P(("group", "dev"), None),
            P("dev", None),
        ),
        out_specs=(P(("group", "dev"), None), P("dev", None), P(), P(), P()),
        check_vma=False,
    )
```
